512 devices in a mesh: section: 8 (over y, core), row: 4 (over x), col: 16 (over z).
Axes of the slice: x: 4, y: 4, z: 16, core: 2. Of those that a mesh axis runs over, the one named last changes fastest.
Arguments:
- weights: bfloat16 [8192, 106496], P('row', ('section', 'col')), may hold values from -12 to 12
- sketch: bfloat16 [106496, 256], P(('section', 'col')), may hold values from -100 to 100
Outputs:
- shared_basis: bfloat16 [8192, 256], P('row')
- coefficients: float32 [256, 106496], P('row', ('section', 'col'))
The draws below stay inside these ranges and needn't reach their ends.
All inputs are finite; a program needn't handle non-finite values.
Results may differ from the reference program's by a relative error of at most 0.0027.
Values may be sent and summed in bfloat16 or wider, within the bound.
A program may use at most 64 MiB of HBM per device.

```python
import math
import jax
import jax.numpy as jnp
from jax import lax

D = 8192
FF = 26624
R = 256
LAYERS = 4


def draw_weights(key, part):
    key = jax.random.fold_in(key, 11)
    order_key, value_key = jax.random.split(key)
    ranks = jax.random.permutation(order_key, D).astype(jnp.float32)
    top_scale = 10.0
    values = jnp.clip(jax.random.normal(value_key, (D, LAYERS * FF), jnp.float32), -4.0, 4.0)
    row_scale = top_scale ** (ranks / (D - 1))
    return (0.3 * row_scale[:, None] * values).astype(jnp.bfloat16)


def draw_sketch(key, part):
    key = jax.random.fold_in(key, 23)
    order_key, base_key, common_key, tilt_key = jax.random.split(key, 4)
    ranks = jax.random.permutation(order_key, R).astype(jnp.float32)
    top_scale = 10.0
    weight_common = 0.8
    base_values = jnp.clip(jax.random.normal(base_key, (LAYERS * FF, R), jnp.float32), -4.0, 4.0)
    common_values = jnp.clip(jax.random.normal(common_key, (LAYERS * FF,), jnp.float32), -4.0, 4.0)
    tilt_values = jax.random.uniform(tilt_key, (R,), jnp.float32, 0.5, 1.5)
    column_scale = top_scale ** (ranks / (R - 1))
    values = column_scale[None, :] * (base_values + weight_common * common_values[:, None] * tilt_values[None, :])
    return values.astype(jnp.bfloat16)


def setup_inputs(seed: int = 0) -> dict:
    keys = jax.random.split(jax.random.key(seed), 3)
    weights = draw_weights(jax.random.fold_in(keys[2], 71), 0)
    sketch = draw_sketch(jax.random.fold_in(keys[2], 71), 0)
    return dict(weights=weights, sketch=sketch)


def reference(weights, sketch):
    sample = jnp.zeros((D, R), jnp.float32)
    for layer_index in range(LAYERS):
        columns = weights[:, layer_index * FF:(layer_index + 1) * FF]
        sketch_rows = sketch[layer_index * FF:(layer_index + 1) * FF]
        sample = sample + jnp.dot(columns.astype(jnp.float32), sketch_rows.astype(jnp.float32), preferred_element_type=jnp.float32)
    gram_matrix = jnp.dot(sample.T, sample, precision=lax.Precision.HIGHEST)
    lower_factor = jnp.linalg.cholesky(gram_matrix)
    identity = jnp.eye(R, dtype=jnp.float32)
    inverse_factor = jax.scipy.linalg.solve_triangular(lower_factor, identity, lower=True)
    shared_basis = (math.sqrt(D) * jnp.dot(sample, inverse_factor.T, precision=lax.Precision.HIGHEST)).astype(jnp.bfloat16)
    coefficient_blocks = []
    for layer_index in range(LAYERS):
        columns = weights[:, layer_index * FF:(layer_index + 1) * FF]
        coefficient_blocks.append(jnp.dot(shared_basis.T.astype(jnp.float32), columns.astype(jnp.float32), preferred_element_type=jnp.float32) / math.sqrt(D))
    return (shared_basis, jnp.concatenate(coefficient_blocks, axis=1))
```

```python
import functools
import math

import jax
import jax.numpy as jnp
from jax import lax
from jax.experimental import pallas as pl
from jax.experimental.pallas import tpu as pltpu
from jax.sharding import PartitionSpec as P

D = 8192
R = 256
MESH = pl.DeviceIdType.MESH


def sum_and_gram(w_hbm, s_ref, hi_out, lo_out, gram_out, w_ref, part, core_in, core_sum, y_in, y_sum, z_in, mine,
                 high, low, gram_part, gram_in, gram_all,
                 w_sem, core_ss, core_rs, y_ss, y_rs, z_ss, z_rs, hz_ss, hz_rs, hy_ss, hy_rs, hc_ss, hc_rs,
                 g_ss, g_rs, b_ss, b_rs, out_sem):
    section = lax.axis_index("section")
    row = lax.axis_index("row")
    col = lax.axis_index("col")
    core = lax.rem(section, 2)
    y = section // 2
    other = 1 - core
    sibling = {"section": 2 * y + other}

    def y_of(k):
        return lax.rem(y + k, 4)

    def z_of(k):
        return lax.rem(col + k, 16)

    def to_y(k):
        return {"section": 2 * y_of(k) + core}

    def to_z(k):
        return {"col": z_of(k)}

    def group_of(k):
        return lax.rem(row + k // 8, 4), lax.rem(section + k % 8, 8)

    def to_group(k):
        r, s = group_of(k)
        return {"row": r, "section": s}

    def send(src, dst, ss, rs, device):
        copy = pltpu.make_async_remote_copy(
            src_ref=src, dst_ref=dst, send_sem=ss, recv_sem=rs, device_id=device, device_id_type=MESH)
        copy.start()
        return copy

    loads = []
    for half in range(2):
        first = jnp.where(half == 0, other, core) * 1024
        load = pltpu.make_async_copy(
            w_hbm.at[pl.ds(pl.multiple_of(first, 1024), 1024)], w_ref.at[half], w_sem.at[half])
        load.start()
        loads.append(load)

    barrier = pltpu.get_barrier_semaphore()
    for k in range(1, 32):
        pl.semaphore_signal(barrier, inc=1, device_id=to_group(k), device_id_type=MESH)
    for k in range(1, 16):
        pl.semaphore_signal(barrier, inc=1, device_id=to_z(k), device_id_type=MESH)

    sent = []
    for half in range(2):
        loads[half].wait()

        @pl.loop(0, 4)
        def _(q):
            rows = pl.ds(pl.multiple_of(q * 256, 256), 256)
            product = jnp.dot(w_ref[half, rows, :], s_ref[...], preferred_element_type=jnp.float32)
            part[half, q] = product.reshape(16, 2, 8, R)

        if half == 0:
            pl.semaphore_wait(barrier, 46)
            core_copies = [
                send(part.at[0, :, :, p], core_in.at[p], core_ss.at[p], core_rs.at[p], sibling) for p in range(2)]
            sent += core_copies

    y_copies = []
    for p in range(2):
        core_copies[p].wait_recv()
        core_sum[p] = part[1, :, :, p] + core_in[p]
        copies = [
            send(core_sum.at[p, y_of(k)], y_in.at[p, k - 1], y_ss.at[p, k - 1], y_rs.at[p, k - 1], to_y(k))
            for k in (2, 1, 3)]
        y_copies.append(copies)
        sent += copies
    z_copies = []
    for p in range(2):
        for copy in y_copies[p]:
            copy.wait_recv()
        y_sum[p] = core_sum[p, y] + y_in[p, 0] + y_in[p, 1] + y_in[p, 2]
        copies = [
            send(y_sum.at[p, z_of(k)], z_in.at[p, k - 1], z_ss.at[p, k - 1], z_rs.at[p, k - 1], to_z(k))
            for k in (8, 7, 9, 6, 10, 5, 11, 4, 12, 3, 13, 2, 14, 1, 15)]
        z_copies.append(copies)
        sent += copies
    for p in range(2):
        for copy in z_copies[p]:
            copy.wait_recv()
        total = y_sum[p, col]
        for k in range(15):
            total = total + z_in[p, k]
        mine[p] = total
    rows16 = mine[...].reshape(16, R)
    rows_hi = rows16.astype(jnp.bfloat16)
    rows_lo = (rows16 - rows_hi.astype(jnp.float32)).astype(jnp.bfloat16)
    high[core, y, col] = rows_hi
    low[core, y, col] = rows_lo
    gathers = []
    for which, ref in enumerate((high, low)):
        copies = [
            send(ref.at[core, y, col], ref.at[core, y, col], hz_ss.at[which, k - 1], hz_rs.at[which, k - 1], to_z(k))
            for k in (8, 7, 9, 6, 10, 5, 11, 4, 12, 3, 13, 2, 14, 1, 15)]
        gathers.append(copies)
        sent += copies

    def spread(which, ref):
        for copy in gathers[which]:
            copy.wait_recv()
        return [
            send(ref.at[core, y], ref.at[core, y], hy_ss.at[which, k - 1], hy_rs.at[which, k - 1], to_y(k))
            for k in (2, 1, 3)]

    spreads = [spread(0, high)]
    sent += spreads[0]
    block = high[core, y].reshape(256, R)
    gram_part[...] = lax.dot_general(
        block, block, (((0,), (0,)), ((), ())), preferred_element_type=jnp.float32).reshape(4, 8, 8, R)
    gram_copies = []
    for k in range(1, 32):
        r, s = group_of(k)
        gram_copies.append(
            send(gram_part.at[r, s], gram_in.at[k - 1], g_ss.at[k - 1], g_rs.at[k - 1], to_group(k)))
    sent += gram_copies
    total = gram_part[row, section]
    for k in range(31):
        gram_copies[k].wait_recv()
        total = total + gram_in[k]
    gram_all[row, section] = total
    back_copies = [
        send(gram_all.at[row, section], gram_all.at[row, section], b_ss.at[k - 1], b_rs.at[k - 1], to_group(k))
        for k in range(1, 32)]
    sent += back_copies

    spreads.append(spread(1, low))
    sent += spreads[1]
    pairs = []
    for which, ref in enumerate((high, low)):
        for copy in spreads[which]:
            copy.wait_recv()
        pairs.append(send(ref.at[core], ref.at[core], hc_ss.at[which], hc_rs.at[which], sibling))
    sent += pairs
    for copy in back_copies:
        copy.wait_recv()
    gram_out[...] = gram_all[...].reshape(R, R)
    for copy in pairs:
        copy.wait_recv()
    outs = [
        pltpu.make_async_copy(high, hi_out, out_sem.at[0]),
        pltpu.make_async_copy(low, lo_out, out_sem.at[1]),
    ]
    for copy in outs:
        copy.start()
    for copy in sent:
        copy.wait_send()
    for copy in outs:
        copy.wait()


def summed(weights, sketch):
    f32, bf16, dma = jnp.float32, jnp.bfloat16, pltpu.SemaphoreType.DMA
    vmem = pl.BlockSpec(memory_space=pltpu.VMEM)
    hbm = pl.BlockSpec(memory_space=pl.ANY)
    full = jax.ShapeDtypeStruct((2, 4, 16, 16, R), bf16)
    return pl.pallas_call(
        sum_and_gram,
        out_shape=(full, full, jax.ShapeDtypeStruct((R, R), f32)),
        in_specs=[hbm, vmem],
        out_specs=(hbm, hbm, vmem),
        scratch_shapes=[
            pltpu.VMEM((2, 1024, 832), bf16),
            pltpu.VMEM((2, 4, 16, 2, 8, R), f32),
            pltpu.VMEM((2, 4, 16, 8, R), f32),
            pltpu.VMEM((2, 4, 16, 8, R), f32),
            pltpu.VMEM((2, 3, 16, 8, R), f32),
            pltpu.VMEM((2, 16, 8, R), f32),
            pltpu.VMEM((2, 15, 8, R), f32),
            pltpu.VMEM((2, 8, R), f32),
            pltpu.VMEM((2, 4, 16, 16, R), bf16),
            pltpu.VMEM((2, 4, 16, 16, R), bf16),
            pltpu.VMEM((4, 8, 8, R), f32),
            pltpu.VMEM((31, 8, R), f32),
            pltpu.VMEM((4, 8, 8, R), f32),
            dma((2,)), dma((2,)), dma((2,)), dma((2, 3)), dma((2, 3)), dma((2, 15)), dma((2, 15)),
            dma((2, 15)), dma((2, 15)), dma((2, 3)), dma((2, 3)), dma((2,)), dma((2,)),
            dma((31,)), dma((31,)), dma((31,)), dma((31,)), dma((2,)),
        ],
        compiler_params=pltpu.CompilerParams(
            collective_id=0, has_side_effects=True, vmem_limit_bytes=48 << 20),
    )(weights, sketch)


def invert_lower(gram_matrix):
    lower_factor = jnp.linalg.cholesky(gram_matrix)
    identity = jnp.eye(gram_matrix.shape[0], dtype=jnp.float32)
    return jax.scipy.linalg.solve_triangular(lower_factor, identity, lower=True)


def shards(weights, sketch):
    high, low, gram_matrix = summed(weights, sketch)
    sample = high.reshape(2048, R).astype(jnp.float32) + low.reshape(2048, R).astype(jnp.float32)
    inverse_factor = invert_lower(gram_matrix)
    product = jnp.dot(sample, inverse_factor.T, precision=lax.Precision.HIGHEST)
    shared_basis = (math.sqrt(D) * product).astype(jnp.bfloat16)
    product = lax.dot_general(
        shared_basis, weights, (((0,), (0,)), ((), ())), preferred_element_type=jnp.float32
    )
    coefficients = lax.psum_scatter(product / math.sqrt(D), "row", scatter_dimension=0, tiled=True)
    return (shared_basis, coefficients)


def solution(mesh):
    placed = (P("row", ("section", "col")), P(("section", "col"), None))
    return jax.shard_map(
        shards,
        mesh=mesh,
        in_specs=placed,
        out_specs=(P("row", None), P("row", ("section", "col"))),
        check_vma=False,
    )
```

```python
import math

import jax
import jax.numpy as jnp
from jax import lax
from jax.experimental import pallas as pl
from jax.experimental.pallas import tpu as pltpu
from jax.sharding import PartitionSpec as P

D = 8192
R = 256
WIDTH = 832
PAD = 896
PANEL = 32
PIECES = ((0, 256), (256, 256), (512, 320))
FAR_FIRST = (8, 7, 9, 6, 10, 5, 11, 4, 12, 3, 13, 2, 14, 1, 15)
MESH = pl.DeviceIdType.MESH
NT = (((1,), (1,)), ((), ()))


def split(x):
    high = x.astype(jnp.bfloat16)
    return high, (x - high.astype(jnp.float32)).astype(jnp.bfloat16)


def spread_lane(x, lane):
    return jnp.take_along_axis(x, jnp.full((8, 128), lane, jnp.int32), axis=1)


def factor_half(half, a, left, right):
    lane = lax.broadcasted_iota(jnp.int32, (8, 128), 1)
    sub = lax.broadcasted_iota(jnp.int32, (8, 128), 0)
    lane256 = lax.broadcasted_iota(jnp.int32, (PANEL, R), 1)
    sub256 = lax.broadcasted_iota(jnp.int32, (PANEL, R), 0)
    lanes = lax.broadcasted_iota(jnp.int32, (R, R), 1)
    subs = lax.broadcasted_iota(jnp.int32, (R, R), 0)
    groups = PANEL // 8
    mine, rest = slice(half * 128, half * 128 + 128), slice((1 - half) * 128, (1 - half) * 128 + 128)

    @pl.loop(0, 128 // PANEL)
    def _(q):
        base = half * 128 + q * PANEL
        rows = pl.ds(pl.multiple_of(base, PANEL), PANEL)
        factors = right[...]
        panel = jnp.where((lane256 >= base - PANEL) & (lane256 < base), 0.0, a[rows, :]) - jnp.dot(
            left[rows, :], factors, preferred_element_type=jnp.float32)
        old = (lanes >= base - PANEL) & (lanes < base) & (subs >= base)
        below = jnp.where(old, 0.0, a[...]) - jnp.dot(left[...], factors, preferred_element_type=jnp.float32)
        x = [panel[8 * g:8 * g + 8, mine] for g in range(groups)]
        z = [panel[8 * g:8 * g + 8, rest] for g in range(groups)]
        for b in range(groups):
            lane0 = q * PANEL + 8 * b
            inside = (lane >= lane0) & (lane < lane0 + 8)
            columns = {g: [spread_lane(x[g], lane0 + j) for j in range(8)] for g in range(b, groups)}
            s = {}
            for j in range(8):
                for i in range(j, 8):
                    s[i, j] = jnp.broadcast_to(columns[b][j][i:i + 1, :], (8, 128))
            u, v = [], []
            for i in range(8):
                spread = jnp.broadcast_to(x[b][i:i + 1, :], (8, 128))
                u.append(jnp.where(inside, jnp.where(lane == lane0 + i, 1.0, 0.0), spread))
                v.append(jnp.broadcast_to(z[b][i:i + 1, :], (8, 128)))
            for g in range(b + 1, groups):
                x[g] = jnp.where(inside, 0.0, x[g])
            for j in range(8):
                scale = lax.rsqrt(s[j, j])
                for i in range(j + 1, 8):
                    s[i, j] = s[i, j] * scale
                for i in range(j + 1, 8):
                    for k in range(j + 1, i + 1):
                        s[i, k] = s[i, k] - s[i, j] * s[k, j]
                u[j] = u[j] * scale
                v[j] = v[j] * scale
                for i in range(j + 1, 8):
                    u[i] = u[i] - s[i, j] * u[j]
                    v[i] = v[i] - s[i, j] * v[j]
                for g in range(b + 1, groups):
                    multiplier = columns[g][j] * scale
                    for k in range(j + 1, 8):
                        columns[g][k] = columns[g][k] - multiplier * s[k, j]
                    x[g] = x[g] - multiplier * u[j]
                    z[g] = z[g] - multiplier * v[j]
            x[b], z[b] = u[0], v[0]
            for i in range(1, 8):
                x[b] = jnp.where(sub == i, u[i], x[b])
                z[b] = jnp.where(sub == i, v[i], z[b])
        parts = [jnp.concatenate(x, axis=0), jnp.concatenate(z, axis=0)]
        new = jnp.concatenate(parts if half == 0 else parts[::-1], axis=1)
        a[...] = below
        a[rows, :] = new
        high, low = split(jnp.where((lane256 > base + sub256) & (lane256 < base + PANEL), 0.0, new))
        right[0:PANEL, :] = high
        right[PANEL:2 * PANEL, :] = low
        right[2 * PANEL:, :] = high
        high, low = split(jnp.where(lane256 >= base + PANEL, new, 0.0).T)
        left[:, 0:PANEL] = high
        left[:, PANEL:2 * PANEL] = high
        left[:, 2 * PANEL:] = low


def whole(w_hbm, s_ref, basis_out, coef_out, w_ref, st_ref, part, core_in, core_sum, y_in, y_sum, z_in, mine,
          high, low, gram_part, gram_in, gram_all, a, left, right, basis_t, coef, coef_send, coef_in,
          w_sem, core_ss, core_rs, y_ss, y_rs, z_ss, z_rs, hz_ss, hz_rs, hy_ss, hy_rs, hc_ss, hc_rs,
          g_ss, g_rs, b_ss, b_rs, c_ss, c_rs):
    section = lax.axis_index("section")
    row = lax.axis_index("row")
    col = lax.axis_index("col")
    core = lax.rem(section, 2)
    y = section // 2
    other = 1 - core
    sibling = {"section": 2 * y + other}

    def y_of(k):
        return lax.rem(y + k, 4)

    def z_of(k):
        return lax.rem(col + k, 16)

    def x_of(k):
        return lax.rem(row + k, 4)

    def to_y(k):
        return {"section": 2 * y_of(k) + core}

    def to_z(k):
        return {"col": z_of(k)}

    def group_of(k):
        return lax.rem(row + k // 8, 4), lax.rem(section + k % 8, 8)

    def to_group(k):
        r, s = group_of(k)
        return {"row": r, "section": s}

    sent = []

    def send(src, dst, ss, rs, device):
        copy = pltpu.make_async_remote_copy(
            src_ref=src, dst_ref=dst, send_sem=ss, recv_sem=rs, device_id=device, device_id_type=MESH)
        copy.start()
        sent.append(copy)
        return copy

    loads = []
    for half, which in enumerate((other, core)):
        load = pltpu.make_async_copy(
            w_hbm.at[:, pl.ds(pl.multiple_of(which * 1024, 1024), 1024)], w_ref.at[which], w_sem.at[half])
        load.start()
        loads.append(load)

    barrier = pltpu.get_barrier_semaphore()
    for k in range(1, 32):
        pl.semaphore_signal(barrier, inc=1, device_id=to_group(k), device_id_type=MESH)
    for k in range(1, 16):
        pl.semaphore_signal(barrier, inc=1, device_id=to_z(k), device_id_type=MESH)

    st_ref[...] = s_ref[...].T
    for half, which in enumerate((other, core)):
        loads[half].wait()
        for q in range(4):
            product = jnp.dot(
                st_ref[...], w_ref[which, :, q * 256:q * 256 + 256], preferred_element_type=jnp.float32)
            part[half, q] = product.reshape(16, 2, 8, R)
        if half == 0:
            pl.semaphore_wait(barrier, 46)
            core_copies = [
                send(part.at[0, :, :, p], core_in.at[p], core_ss.at[p], core_rs.at[p], sibling) for p in range(2)]

    y_copies = []
    for p in range(2):
        core_copies[p].wait_recv()
        core_sum[p] = part[1, :, :, p] + core_in[p]
        y_copies.append([
            send(core_sum.at[p, y_of(k)], y_in.at[p, k - 1], y_ss.at[p, k - 1], y_rs.at[p, k - 1], to_y(k))
            for k in (2, 1, 3)])
    z_copies = []
    for p in range(2):
        for copy in y_copies[p]:
            copy.wait_recv()
        y_sum[p] = core_sum[p, y] + y_in[p, 0] + y_in[p, 1] + y_in[p, 2]
        z_copies.append([
            send(y_sum.at[p, z_of(k)], z_in.at[p, k - 1], z_ss.at[p, k - 1], z_rs.at[p, k - 1], to_z(k))
            for k in FAR_FIRST])
    for p in range(2):
        for copy in z_copies[p]:
            copy.wait_recv()
        total = y_sum[p, col]
        for k in range(15):
            total = total + z_in[p, k]
        mine[p] = total
    high[core, y, col], low[core, y, col] = split(mine[...].reshape(16, R))
    gathers = [
        [send(ref.at[core, y, col], ref.at[core, y, col], hz_ss.at[which, k - 1], hz_rs.at[which, k - 1], to_z(k))
         for k in FAR_FIRST]
        for which, ref in enumerate((high, low))]

    def spread(which, ref):
        return [
            send(ref.at[core, y], ref.at[core, y], hy_ss.at[which, k - 1], hy_rs.at[which, k - 1], to_y(k))
            for k in (2, 1, 3)]

    def pair(which, ref):
        return send(ref.at[core], ref.at[core], hc_ss.at[which], hc_rs.at[which], sibling)

    def arrive(copies):
        for copy in copies:
            copy.wait_recv()

    arrive(gathers[0])
    block = high[core, y].reshape(R, R)
    gram_part[...] = lax.dot_general(block, block, NT, preferred_element_type=jnp.float32).reshape(4, 8, 8, R)
    gram_copies = []
    for k in range(1, 32):
        r, s = group_of(k)
        gram_copies.append(
            send(gram_part.at[r, s], gram_in.at[k - 1], g_ss.at[k - 1], g_rs.at[k - 1], to_group(k)))
    spread_high = spread(0, high)
    total = gram_part[row, section]
    for k in range(31):
        gram_copies[k].wait_recv()
        total = total + gram_in[k]
    gram_all[row, section] = total
    back_copies = [
        send(gram_all.at[row, section], gram_all.at[row, section], b_ss.at[k - 1], b_rs.at[k - 1], to_group(k))
        for k in range(1, 32)]

    arrive(gathers[1])
    spread_low = spread(1, low)
    coef_send[:, :, 768:] = jnp.zeros((4, 64, PAD - 768), jnp.bfloat16)
    left[...] = jnp.zeros_like(left)
    right[...] = jnp.zeros_like(right)
    arrive(spread_high)
    pair_high = pair(0, high)
    arrive(back_copies)
    a[...] = gram_all[...].reshape(R, R)
    factor_half(0, a, left, right)
    arrive(spread_low)
    pair_low = pair(1, low)
    factor_half(1, a, left, right)

    lower = lax.broadcasted_iota(jnp.int32, (R, R), 0) >= lax.broadcasted_iota(jnp.int32, (R, R), 1)
    inverse_high, inverse_low = split(jnp.where(lower, a[...] * math.sqrt(D), 0.0))
    arrive([pair_high, pair_low])

    def dot(p, q):
        return jnp.dot(p, q, preferred_element_type=jnp.float32)

    for c in range(2):
        for q in range(4):
            block_high = high[c, q].reshape(R, R)
            block_low = low[c, q].reshape(R, R)
            product = dot(inverse_high, block_high) + (dot(inverse_high, block_low) + dot(inverse_low, block_high))
            basis_t[c, :, q * 256:q * 256 + 256] = product.astype(jnp.bfloat16)
    coef_copies = []
    for piece, (first, width) in enumerate(PIECES):
        product = jnp.zeros((R, width), jnp.float32)
        for c in range(2):
            product = product + lax.dot_general(
                basis_t[c], w_ref[c, first:first + width, :], NT, preferred_element_type=jnp.float32)
        product = product.reshape(4, 64, width)
        coef[:, :, first:first + width] = product
        coef_send[:, :, first:first + width] = product.astype(jnp.bfloat16)
        lanes = pl.ds(first, width if piece < 2 else PAD - first)
        coef_copies.append([
            send(coef_send.at[x_of(k), :, lanes], coef_in.at[k - 1, :, lanes], c_ss.at[piece, k - 1],
                 c_rs.at[piece, k - 1], {"row": x_of(k)})
            for k in (2, 1, 3)])
    for c in range(2):
        for q in range(4):
            first = c * 1024 + q * 256
            basis_out[first:first + 256, :] = basis_t[c, :, q * 256:q * 256 + 256].T
    for piece, (first, width) in enumerate(PIECES):
        arrive(coef_copies[piece])
        total = coef[row, :, first:first + width]
        for k in range(3):
            total = total + coef_in[k, :, first:first + width].astype(jnp.float32)
        coef_out[:, first:first + width] = total / math.sqrt(D)
    for copy in sent:
        copy.wait_send()


def shards(weights, sketch):
    f32, bf16, dma = jnp.float32, jnp.bfloat16, pltpu.SemaphoreType.DMA
    vmem = pl.BlockSpec(memory_space=pltpu.VMEM)
    return pl.pallas_call(
        whole,
        out_shape=(jax.ShapeDtypeStruct((2048, R), bf16), jax.ShapeDtypeStruct((64, WIDTH), f32)),
        in_specs=[pl.BlockSpec(memory_space=pl.ANY), vmem],
        out_specs=(vmem, vmem),
        scratch_shapes=[
            pltpu.VMEM((2, WIDTH, 1024), bf16),
            pltpu.VMEM((R, WIDTH), bf16),
            pltpu.VMEM((2, 4, 16, 2, 8, R), f32),
            pltpu.VMEM((2, 4, 16, 8, R), f32),
            pltpu.VMEM((2, 4, 16, 8, R), f32),
            pltpu.VMEM((2, 3, 16, 8, R), f32),
            pltpu.VMEM((2, 16, 8, R), f32),
            pltpu.VMEM((2, 15, 8, R), f32),
            pltpu.VMEM((2, 8, R), f32),
            pltpu.VMEM((2, 4, 16, 16, R), bf16),
            pltpu.VMEM((2, 4, 16, 16, R), bf16),
            pltpu.VMEM((4, 8, 8, R), f32),
            pltpu.VMEM((31, 8, R), f32),
            pltpu.VMEM((4, 8, 8, R), f32),
            pltpu.VMEM((R, R), f32),
            pltpu.VMEM((R, 3 * PANEL), bf16),
            pltpu.VMEM((3 * PANEL, R), bf16),
            pltpu.VMEM((2, R, 1024), bf16),
            pltpu.VMEM((4, 64, WIDTH), f32),
            pltpu.VMEM((4, 64, PAD), bf16),
            pltpu.VMEM((3, 64, PAD), bf16),
            dma((2,)), dma((2,)), dma((2,)), dma((2, 3)), dma((2, 3)), dma((2, 15)), dma((2, 15)),
            dma((2, 15)), dma((2, 15)), dma((2, 3)), dma((2, 3)), dma((2,)), dma((2,)),
            dma((31,)), dma((31,)), dma((31,)), dma((31,)), dma((3, 3)), dma((3, 3)),
        ],
        compiler_params=pltpu.CompilerParams(
            collective_id=0, has_side_effects=True, vmem_limit_bytes=60 << 20),
    )(weights.T, sketch)


def solution(mesh):
    placed = (P("row", ("section", "col")), P(("section", "col"), None))
    return jax.shard_map(
        shards,
        mesh=mesh,
        in_specs=placed,
        out_specs=(P("row", None), P("row", ("section", "col"))),
        check_vma=False,
    )
```

```python
import math

import jax
import jax.numpy as jnp
from jax import lax
from jax.experimental import pallas as pl
from jax.experimental.pallas import tpu as pltpu
from jax.sharding import PartitionSpec as P

D = 8192
R = 256
WIDTH = 832
PAD = 896
PANEL = 64
PIECES = ((0, 256), (256, 256), (512, 320))
QUARTERS = ((0, 0), (0, 1), (1, 0), (1, 1))
GROUP = tuple(sorted(range(1, 32), key=lambda k: -(2 * min(k // 8, 4 - k // 8) + min(k % 8, 8 - k % 8))))
FAR_FIRST = (8, 7, 9, 6, 10, 5, 11, 4, 12, 3, 13, 2, 14, 1, 15)
MESH = pl.DeviceIdType.MESH
NT = (((1,), (1,)), ((), ()))


def split(x):
    high = x.astype(jnp.bfloat16)
    return high, (x - high.astype(jnp.float32)).astype(jnp.bfloat16)


def spread_lane(x, lane):
    return jnp.take_along_axis(x, jnp.full((8, 128), lane, jnp.int32), axis=1)


def factor_half(half, a, left, right):
    lane = lax.broadcasted_iota(jnp.int32, (8, 128), 1)
    sub = lax.broadcasted_iota(jnp.int32, (8, 128), 0)
    lane256 = lax.broadcasted_iota(jnp.int32, (PANEL, R), 1)
    sub256 = lax.broadcasted_iota(jnp.int32, (PANEL, R), 0)
    lanes = lax.broadcasted_iota(jnp.int32, (R, R), 1)
    subs = lax.broadcasted_iota(jnp.int32, (R, R), 0)
    groups = PANEL // 8
    mine, rest = slice(half * 128, half * 128 + 128), slice((1 - half) * 128, (1 - half) * 128 + 128)

    @pl.loop(0, 128 // PANEL)
    def _(q):
        base = half * 128 + q * PANEL
        rows = pl.ds(pl.multiple_of(base, PANEL), PANEL)
        factors = right[...]
        panel = jnp.where((lane256 >= base - PANEL) & (lane256 < base), 0.0, a[rows, :]) - jnp.dot(
            left[rows, :], factors, preferred_element_type=jnp.float32)
        old = (lanes >= base - PANEL) & (lanes < base) & (subs >= base)
        below = jnp.where(old, 0.0, a[...]) - jnp.dot(left[...], factors, preferred_element_type=jnp.float32)
        x = [panel[8 * g:8 * g + 8, mine] for g in range(groups)]
        z = [panel[8 * g:8 * g + 8, rest] for g in range(groups)]
        for b in range(groups):
            lane0 = q * PANEL + 8 * b
            inside = (lane >= lane0) & (lane < lane0 + 8)
            columns = {g: [spread_lane(x[g], lane0 + j) for j in range(8)] for g in range(b, groups)}
            s = {}
            for j in range(8):
                for i in range(j, 8):
                    s[i, j] = jnp.broadcast_to(columns[b][j][i:i + 1, :], (8, 128))
            u, v = [], []
            for i in range(8):
                spread = jnp.broadcast_to(x[b][i:i + 1, :], (8, 128))
                u.append(jnp.where(inside, jnp.where(lane == lane0 + i, 1.0, 0.0), spread))
                v.append(jnp.broadcast_to(z[b][i:i + 1, :], (8, 128)))
            for g in range(b + 1, groups):
                x[g] = jnp.where(inside, 0.0, x[g])
            for j in range(8):
                scale = lax.rsqrt(s[j, j])
                for i in range(j + 1, 8):
                    s[i, j] = s[i, j] * scale
                for i in range(j + 1, 8):
                    for k in range(j + 1, i + 1):
                        s[i, k] = s[i, k] - s[i, j] * s[k, j]
                u[j] = u[j] * scale
                v[j] = v[j] * scale
                for i in range(j + 1, 8):
                    u[i] = u[i] - s[i, j] * u[j]
                    v[i] = v[i] - s[i, j] * v[j]
                for g in range(b + 1, groups):
                    multiplier = columns[g][j] * scale
                    for k in range(j + 1, 8):
                        columns[g][k] = columns[g][k] - multiplier * s[k, j]
                    x[g] = x[g] - multiplier * u[j]
                    z[g] = z[g] - multiplier * v[j]
            x[b], z[b] = u[0], v[0]
            for i in range(1, 8):
                x[b] = jnp.where(sub == i, u[i], x[b])
                z[b] = jnp.where(sub == i, v[i], z[b])
        parts = [jnp.concatenate(x, axis=0), jnp.concatenate(z, axis=0)]
        new = jnp.concatenate(parts if half == 0 else parts[::-1], axis=1)
        a[...] = below
        a[rows, :] = new
        high, low = split(jnp.where((lane256 > base + sub256) & (lane256 < base + PANEL), 0.0, new))
        right[0:PANEL, :] = high
        right[PANEL:2 * PANEL, :] = low
        right[2 * PANEL:, :] = high
        high, low = split(jnp.where(lane256 >= base + PANEL, new, 0.0).T)
        left[:, 0:PANEL] = high
        left[:, PANEL:2 * PANEL] = high
        left[:, 2 * PANEL:] = low


def whole(w_hbm, s_hbm, basis_out, coef_out, w_ref, s_ref, st_ref, part, core_in, core_sum, y_in, y_sum, z_in,
          rows, gram_part, gram_in, gram_all, a, left, right, basis_t, coef, coef_send, coef_in,
          w_sem, core_ss, core_rs, y_ss, y_rs, z_ss, z_rs, h_ss, h_rs, hy_ss, hy_rs, hc_ss, hc_rs,
          g_ss, g_rs, b_ss, b_rs, c_ss, c_rs):
    section = lax.axis_index("section")
    row = lax.axis_index("row")
    col = lax.axis_index("col")
    core = lax.rem(section, 2)
    y = section // 2
    other = 1 - core
    sibling = {"section": 2 * y + other}

    def y_of(k):
        return lax.rem(y + k, 4)

    def z_of(k):
        return lax.rem(col + k, 16)

    def x_of(k):
        return lax.rem(row + k, 4)

    def to_y(k):
        return {"section": 2 * y_of(k) + core}

    def to_z(k):
        return {"col": z_of(k)}

    def group_of(k):
        return lax.rem(row + k // 8, 4), lax.rem(section + k % 8, 8)

    def to_group(k):
        r, s = group_of(k)
        return {"row": r, "section": s}

    sent, pending = [], []

    def send(src, dst, ss, rs, device):
        copy = pltpu.make_async_remote_copy(
            src_ref=src, dst_ref=dst, send_sem=ss, recv_sem=rs, device_id=device, device_id_type=MESH)
        copy.start()
        sent.append(copy)
        pending.append(copy)
        return copy

    def arrive(copies):
        for copy in copies:
            copy.wait_recv()
            pending[:] = [c for c in pending if c is not copy]

    barrier = pltpu.get_barrier_semaphore()
    for k in range(1, 32):
        pl.semaphore_signal(barrier, inc=1, device_id=to_group(k), device_id_type=MESH)
    for k in range(1, 16):
        pl.semaphore_signal(barrier, inc=1, device_id=to_z(k), device_id_type=MESH)

    loads, core_copies = [], []
    load_s = pltpu.make_async_copy(s_hbm, s_ref, w_sem.at[2])
    load_s.start()
    for half, which in enumerate((other, core)):
        load = pltpu.make_async_copy(
            w_hbm.at[:, pl.ds(pl.multiple_of(which * 1024, 1024), 1024)], w_ref.at[which], w_sem.at[half])
        load.start()
        loads.append(load)

    load_s.wait()
    st_ref[...] = s_ref[...].T
    for half, which in enumerate((other, core)):
        loads[half].wait()
        for p in range(2):
            product = jnp.dot(
                st_ref[...], w_ref[which, :, p * 512:p * 512 + 512], preferred_element_type=jnp.float32)
            for q in range(4):
                part[half, p, q] = product[:, q * 128:q * 128 + 128].reshape(16, 2, 8, 128)
            if half == 0:
                if p == 0:
                    pl.semaphore_wait(barrier, 46)
                core_copies.append(send(part.at[0, p], core_in.at[p], core_ss.at[p], core_rs.at[p], sibling))
    y_copies = []
    for p, r in QUARTERS:
        if r == 0:
            arrive([core_copies[p]])
        core_sum[p, r] = part[1, p, :, :, r] + core_in[p, :, :, r]
        y_copies.append([
            send(core_sum.at[p, r, y_of(k)], y_in.at[p, r, k - 1], y_ss.at[p, r, k - 1], y_rs.at[p, r, k - 1], to_y(k))
            for k in (2, 1, 3)])
    z_copies = []
    for quarter, (p, r) in enumerate(QUARTERS):
        arrive(y_copies[quarter])
        y_sum[p, r] = core_sum[p, r, y] + y_in[p, r, 0] + y_in[p, r, 1] + y_in[p, r, 2]
        z_copies.append([
            send(y_sum.at[p, r, z_of(k)], z_in.at[p, r, k - 1], z_ss.at[p, r, k - 1], z_rs.at[p, r, k - 1], to_z(k))
            for k in FAR_FIRST])
    gathers = []
    for quarter, (p, r) in enumerate(QUARTERS):
        arrive(z_copies[quarter])
        total = y_sum[p, r, col]
        for k in range(15):
            total = total + z_in[p, r, k]
        rows[core, p, y, col, r] = total
        gathers.append([
            send(rows.at[core, p, y, col, r], rows.at[core, p, y, col, r], h_ss.at[p, r, k - 1], h_rs.at[p, r, k - 1],
                 to_z(k))
            for k in FAR_FIRST])

    def spread(p):
        return [
            send(rows.at[core, p, y], rows.at[core, p, y], hy_ss.at[p, k - 1], hy_rs.at[p, k - 1], to_y(k))
            for k in (2, 1, 3)]

    def pair(p):
        return send(rows.at[core, p], rows.at[core, p], hc_ss.at[p], hc_rs.at[p], sibling)

    gram = jnp.zeros((R, R), jnp.float32)
    spreads = []
    for p in range(2):
        arrive(gathers[2 * p])
        arrive(gathers[2 * p + 1])
        if p == 0:
            spreads.append(spread(0))
        high, low = split(rows[core, p, y].reshape(R, 128))
        gram = gram + (lax.dot_general(high, high, NT, preferred_element_type=jnp.float32) + (
            lax.dot_general(high, low, NT, preferred_element_type=jnp.float32) +
            lax.dot_general(low, high, NT, preferred_element_type=jnp.float32)))
    gram_part[...] = gram.reshape(4, 8, 8, R)
    gram_copies = {}
    for k in GROUP:
        r, s = group_of(k)
        gram_copies[k] = send(gram_part.at[r, s], gram_in.at[k - 1], g_ss.at[k - 1], g_rs.at[k - 1], to_group(k))
    total = gram_part[row, section]
    for k in GROUP[::-1]:
        arrive([gram_copies[k]])
        total = total + gram_in[k - 1]
    gram_all[row, section] = total
    back_copies = [
        send(gram_all.at[row, section], gram_all.at[row, section], b_ss.at[k - 1], b_rs.at[k - 1], to_group(k))
        for k in GROUP]
    spreads.append(spread(1))
    coef_send[:, :, 768:] = jnp.zeros((4, 64, PAD - 768), jnp.bfloat16)
    left[...] = jnp.zeros_like(left)
    right[...] = jnp.zeros_like(right)
    arrive(spreads[0])
    pairs = [pair(0)]
    arrive(back_copies)
    a[...] = gram_all[...].reshape(R, R)
    factor_half(0, a, left, right)
    arrive(spreads[1])
    pairs.append(pair(1))
    factor_half(1, a, left, right)

    lower = lax.broadcasted_iota(jnp.int32, (R, R), 0) >= lax.broadcasted_iota(jnp.int32, (R, R), 1)
    inverse_high, inverse_low = split(jnp.where(lower, a[...] * math.sqrt(D), 0.0))
    arrive(pairs)

    def dot(p, q):
        return jnp.dot(p, q, preferred_element_type=jnp.float32)

    for c in range(2):
        for p in range(2):
            for q in range(0, 4, 2):
                block = jnp.concatenate([rows[c, p, q].reshape(R, 128), rows[c, p, q + 1].reshape(R, 128)], axis=1)
                high, low = split(block)
                product = dot(inverse_high, high) + (dot(inverse_high, low) + dot(inverse_low, high))
                first = p * 512 + q * 128
                basis_t[c, :, first:first + 256] = product.astype(jnp.bfloat16)
    coef_copies = []
    for piece, (first, width) in enumerate(PIECES):
        product = jnp.zeros((R, width), jnp.float32)
        for c in range(2):
            product = product + lax.dot_general(
                basis_t[c], w_ref[c, first:first + width, :], NT, preferred_element_type=jnp.float32)
        product = product.reshape(4, 64, width)
        coef[:, :, first:first + width] = product
        coef_send[:, :, first:first + width] = product.astype(jnp.bfloat16)
        lanes = pl.ds(first, width if piece < 2 else PAD - first)
        coef_copies.append([
            send(coef_send.at[x_of(k), :, lanes], coef_in.at[k - 1, :, lanes], c_ss.at[piece, k - 1],
                 c_rs.at[piece, k - 1], {"row": x_of(k)})
            for k in (2, 1, 3)])
    for c in range(2):
        for q in range(4):
            first = c * 1024 + q * 256
            basis_out[first:first + 256, :] = basis_t[c, :, q * 256:q * 256 + 256].T
    for piece, (first, width) in enumerate(PIECES):
        arrive(coef_copies[piece])
        total = coef[row, :, first:first + width]
        for k in range(3):
            total = total + coef_in[k, :, first:first + width].astype(jnp.float32)
        coef_out[:, first:first + width] = total / math.sqrt(D)
    for copy in sent:
        copy.wait_send()


def shards(weights, sketch):
    f32, bf16, dma = jnp.float32, jnp.bfloat16, pltpu.SemaphoreType.DMA
    vmem = pl.BlockSpec(memory_space=pltpu.VMEM)
    return pl.pallas_call(
        whole,
        out_shape=(jax.ShapeDtypeStruct((2048, R), bf16), jax.ShapeDtypeStruct((64, WIDTH), f32)),
        in_specs=[pl.BlockSpec(memory_space=pltpu.HBM)] * 2,
        out_specs=(vmem, vmem),
        scratch_shapes=[
            pltpu.VMEM((2, WIDTH, 1024), bf16),
            pltpu.VMEM((WIDTH, R), bf16),
            pltpu.VMEM((R, WIDTH), bf16),
            pltpu.VMEM((2, 2, 4, 16, 2, 8, 128), f32),
            pltpu.VMEM((2, 4, 16, 2, 8, 128), f32),
            pltpu.VMEM((2, 2, 4, 16, 8, 128), f32),
            pltpu.VMEM((2, 2, 3, 16, 8, 128), f32),
            pltpu.VMEM((2, 2, 16, 8, 128), f32),
            pltpu.VMEM((2, 2, 15, 8, 128), f32),
            pltpu.VMEM((2, 2, 4, 16, 2, 8, 128), f32),
            pltpu.VMEM((4, 8, 8, R), f32),
            pltpu.VMEM((31, 8, R), f32),
            pltpu.VMEM((4, 8, 8, R), f32),
            pltpu.VMEM((R, R), f32),
            pltpu.VMEM((R, 3 * PANEL), bf16),
            pltpu.VMEM((3 * PANEL, R), bf16),
            pltpu.VMEM((2, R, 1024), bf16),
            pltpu.VMEM((4, 64, WIDTH), f32),
            pltpu.VMEM((4, 64, PAD), bf16),
            pltpu.VMEM((3, 64, PAD), bf16),
            dma((3,)), dma((2,)), dma((2,)), dma((2, 2, 3)), dma((2, 2, 3)), dma((2, 2, 15)), dma((2, 2, 15)),
            dma((2, 2, 15)), dma((2, 2, 15)), dma((2, 3)), dma((2, 3)), dma((2,)), dma((2,)),
            dma((31,)), dma((31,)), dma((31,)), dma((31,)), dma((3, 3)), dma((3, 3)),
        ],
        compiler_params=pltpu.CompilerParams(
            collective_id=0, has_side_effects=True, vmem_limit_bytes=51 << 20),
    )(weights.T, sketch)


def solution(mesh):
    placed = (P("row", ("section", "col")), P(("section", "col"), None))
    return jax.shard_map(
        shards,
        mesh=mesh,
        in_specs=placed,
        out_specs=(P("row", None), P("row", ("section", "col"))),
        check_vma=False,
    )
```

```python
import math

import jax
import jax.numpy as jnp
from jax import lax
from jax.experimental import pallas as pl
from jax.experimental.pallas import tpu as pltpu
from jax.sharding import PartitionSpec as P

D = 8192
R = 256
WIDTH = 832
PAD = 896
PANEL = 64
PIECES = ((0, 256), (256, 256), (512, 320))
QUARTERS = ((0, 0), (0, 1), (1, 0), (1, 1))
GROUP = tuple(sorted(range(1, 32), key=lambda k: -(2 * min(k // 8, 4 - k // 8) + min(k % 8, 8 - k % 8))))
FAR_FIRST = (8, 7, 9, 6, 10, 5, 11, 4, 12, 3, 13, 2, 14, 1, 15)
MESH = pl.DeviceIdType.MESH
NT = (((1,), (1,)), ((), ()))


def split(x):
    high = x.astype(jnp.bfloat16)
    return high, (x - high.astype(jnp.float32)).astype(jnp.bfloat16)


def spread_lane(x, lane):
    return jnp.take_along_axis(x, jnp.full((8, 128), lane, jnp.int32), axis=1)


def factor_half(half, a, left, right):
    lane = lax.broadcasted_iota(jnp.int32, (8, 128), 1)
    sub = lax.broadcasted_iota(jnp.int32, (8, 128), 0)
    lane256 = lax.broadcasted_iota(jnp.int32, (PANEL, R), 1)
    sub256 = lax.broadcasted_iota(jnp.int32, (PANEL, R), 0)
    lanes = lax.broadcasted_iota(jnp.int32, (R, R), 1)
    subs = lax.broadcasted_iota(jnp.int32, (R, R), 0)
    groups = PANEL // 8
    mine, rest = slice(half * 128, half * 128 + 128), slice((1 - half) * 128, (1 - half) * 128 + 128)

    @pl.loop(0, 128 // PANEL)
    def _(q):
        base = half * 128 + q * PANEL
        rows = pl.ds(pl.multiple_of(base, PANEL), PANEL)
        factors = right[...]
        panel = jnp.where((lane256 >= base - PANEL) & (lane256 < base), 0.0, a[rows, :]) - jnp.dot(
            left[rows, :], factors, preferred_element_type=jnp.float32)
        old = (lanes >= base - PANEL) & (lanes < base) & (subs >= base)
        below = jnp.where(old, 0.0, a[...]) - jnp.dot(left[...], factors, preferred_element_type=jnp.float32)
        x = [panel[8 * g:8 * g + 8, mine] for g in range(groups)]
        z = [panel[8 * g:8 * g + 8, rest] for g in range(groups)]
        for b in range(groups):
            lane0 = q * PANEL + 8 * b
            inside = (lane >= lane0) & (lane < lane0 + 8)
            columns = {g: [spread_lane(x[g], lane0 + j) for j in range(8)] for g in range(b, groups)}
            s = {}
            for j in range(8):
                for i in range(j, 8):
                    s[i, j] = jnp.broadcast_to(columns[b][j][i:i + 1, :], (8, 128))
            u, v = [], []
            for i in range(8):
                spread = jnp.broadcast_to(x[b][i:i + 1, :], (8, 128))
                u.append(jnp.where(inside, jnp.where(lane == lane0 + i, 1.0, 0.0), spread))
                v.append(jnp.broadcast_to(z[b][i:i + 1, :], (8, 128)))
            for g in range(b + 1, groups):
                x[g] = jnp.where(inside, 0.0, x[g])
            for j in range(8):
                scale = lax.rsqrt(s[j, j])
                for i in range(j + 1, 8):
                    s[i, j] = s[i, j] * scale
                for i in range(j + 1, 8):
                    for k in range(j + 1, i + 1):
                        s[i, k] = s[i, k] - s[i, j] * s[k, j]
                u[j] = u[j] * scale
                v[j] = v[j] * scale
                for i in range(j + 1, 8):
                    u[i] = u[i] - s[i, j] * u[j]
                    v[i] = v[i] - s[i, j] * v[j]
                for g in range(b + 1, groups):
                    multiplier = columns[g][j] * scale
                    for k in range(j + 1, 8):
                        columns[g][k] = columns[g][k] - multiplier * s[k, j]
                    x[g] = x[g] - multiplier * u[j]
                    z[g] = z[g] - multiplier * v[j]
            x[b], z[b] = u[0], v[0]
            for i in range(1, 8):
                x[b] = jnp.where(sub == i, u[i], x[b])
                z[b] = jnp.where(sub == i, v[i], z[b])
        parts = [jnp.concatenate(x, axis=0), jnp.concatenate(z, axis=0)]
        new = jnp.concatenate(parts if half == 0 else parts[::-1], axis=1)
        a[...] = below
        a[rows, :] = new
        high, low = split(jnp.where((lane256 > base + sub256) & (lane256 < base + PANEL), 0.0, new))
        right[0:PANEL, :] = high
        right[PANEL:2 * PANEL, :] = low
        right[2 * PANEL:, :] = high
        high, low = split(jnp.where(lane256 >= base + PANEL, new, 0.0).T)
        left[:, 0:PANEL] = high
        left[:, PANEL:2 * PANEL] = high
        left[:, 2 * PANEL:] = low


def whole(w_hbm, s_hbm, basis_out, coef_out, w_ref, s_ref, st_ref, part, core_in, core_sum, y_in, y_sum, z_in,
          rows, gram_part, gram_in, gram_all, a, left, right, basis_t, coef, coef_send, coef_in,
          w_sem, core_ss, core_rs, y_ss, y_rs, z_ss, z_rs, h_ss, h_rs, hy_ss, hy_rs, hc_ss, hc_rs,
          g_ss, g_rs, b_ss, b_rs, c_ss, c_rs):
    section = lax.axis_index("section")
    row = lax.axis_index("row")
    col = lax.axis_index("col")
    core = lax.rem(section, 2)
    y = section // 2
    other = 1 - core
    sibling = {"section": 2 * y + other}

    def y_of(k):
        return lax.rem(y + k, 4)

    def z_of(k):
        return lax.rem(col + k, 16)

    def x_of(k):
        return lax.rem(row + k, 4)

    def to_y(k):
        return {"section": 2 * y_of(k) + core}

    def to_z(k):
        return {"col": z_of(k)}

    def group_of(k):
        return lax.rem(row + k // 8, 4), lax.rem(section + k % 8, 8)

    def to_group(k):
        r, s = group_of(k)
        return {"row": r, "section": s}

    sent, pending = [], []

    def send(src, dst, ss, rs, device):
        copy = pltpu.make_async_remote_copy(
            src_ref=src, dst_ref=dst, send_sem=ss, recv_sem=rs, device_id=device, device_id_type=MESH)
        copy.start()
        sent.append(copy)
        pending.append(copy)
        return copy

    def arrive(copies):
        for copy in copies:
            copy.wait_recv()
            pending[:] = [c for c in pending if c is not copy]

    barrier = pltpu.get_barrier_semaphore()
    for k in range(1, 32):
        pl.semaphore_signal(barrier, inc=1, device_id=to_group(k), device_id_type=MESH)
    for k in range(1, 16):
        pl.semaphore_signal(barrier, inc=1, device_id=to_z(k), device_id_type=MESH)

    loads, core_copies = [], []
    load_s = pltpu.make_async_copy(s_hbm, s_ref, w_sem.at[2])
    load_s.start()
    for half, which in enumerate((other, core)):
        load = pltpu.make_async_copy(
            w_hbm.at[:, pl.ds(pl.multiple_of(which * 1024, 1024), 1024)], w_ref.at[which], w_sem.at[half])
        load.start()
        loads.append(load)

    load_s.wait()
    st_ref[...] = s_ref[...].T
    for half, which in enumerate((other, core)):
        loads[half].wait()
        for p in range(2):
            product = jnp.dot(
                st_ref[...], w_ref[which, :, p * 512:p * 512 + 512], preferred_element_type=jnp.float32)
            for q in range(4):
                part[half, p, q] = product[:, q * 128:q * 128 + 128].reshape(16, 2, 8, 128)
            if half == 0:
                if p == 0:
                    pl.semaphore_wait(barrier, 46)
                core_copies += [
                    send(part.at[0, p, :, :, r], core_in.at[p, r], core_ss.at[p, r], core_rs.at[p, r], sibling)
                    for r in range(2)]
    y_copies = []
    for quarter, (p, r) in enumerate(QUARTERS):
        arrive([core_copies[quarter]])
        core_sum[p, r] = part[1, p, :, :, r] + core_in[p, r]
        y_copies.append([
            send(core_sum.at[p, r, y_of(k)], y_in.at[p, r, k - 1], y_ss.at[p, r, k - 1], y_rs.at[p, r, k - 1], to_y(k))
            for k in (2, 1, 3)])
    z_copies = []
    for quarter, (p, r) in enumerate(QUARTERS):
        arrive(y_copies[quarter])
        y_sum[p, r] = core_sum[p, r, y] + y_in[p, r, 0] + y_in[p, r, 1] + y_in[p, r, 2]
        z_copies.append([
            send(y_sum.at[p, r, z_of(k)], z_in.at[p, r, k - 1], z_ss.at[p, r, k - 1], z_rs.at[p, r, k - 1], to_z(k))
            for k in FAR_FIRST])
    gathers = []
    for quarter, (p, r) in enumerate(QUARTERS):
        arrive(z_copies[quarter])
        total = y_sum[p, r, col]
        for k in range(15):
            total = total + z_in[p, r, k]
        rows[core, p, y, col, r] = total
        gathers.append([
            send(rows.at[core, p, y, col, r], rows.at[core, p, y, col, r], h_ss.at[p, r, k - 1], h_rs.at[p, r, k - 1],
                 to_z(k))
            for k in FAR_FIRST])

    def spread(p):
        return [
            send(rows.at[core, p, y], rows.at[core, p, y], hy_ss.at[p, k - 1], hy_rs.at[p, k - 1], to_y(k))
            for k in (2, 1, 3)]

    def pair(p):
        return send(rows.at[core, p], rows.at[core, p], hc_ss.at[p], hc_rs.at[p], sibling)

    gram = jnp.zeros((R, R), jnp.float32)
    spreads = []
    for p in range(2):
        arrive(gathers[2 * p])
        arrive(gathers[2 * p + 1])
        if p == 0:
            spreads.append(spread(0))
        high, low = split(rows[core, p, y].reshape(R, 128))
        gram = gram + (lax.dot_general(high, high, NT, preferred_element_type=jnp.float32) + (
            lax.dot_general(high, low, NT, preferred_element_type=jnp.float32) +
            lax.dot_general(low, high, NT, preferred_element_type=jnp.float32)))
    gram_part[...] = gram.reshape(4, 8, 8, R)
    gram_copies = {}
    for k in GROUP:
        r, s = group_of(k)
        gram_copies[k] = send(gram_part.at[r, s], gram_in.at[k - 1], g_ss.at[k - 1], g_rs.at[k - 1], to_group(k))
    total = gram_part[row, section]
    for k in GROUP[::-1]:
        arrive([gram_copies[k]])
        total = total + gram_in[k - 1]
    gram_all[row, section] = total
    back_copies = [
        send(gram_all.at[row, section], gram_all.at[row, section], b_ss.at[k - 1], b_rs.at[k - 1], to_group(k))
        for k in GROUP]
    spreads.append(spread(1))
    coef_send[:, :, 768:] = jnp.zeros((4, 64, PAD - 768), jnp.bfloat16)
    left[...] = jnp.zeros_like(left)
    right[...] = jnp.zeros_like(right)
    arrive(spreads[0])
    pairs = [pair(0)]
    arrive(back_copies)
    a[...] = gram_all[...].reshape(R, R)
    factor_half(0, a, left, right)
    arrive(spreads[1])
    pairs.append(pair(1))
    factor_half(1, a, left, right)

    lower = lax.broadcasted_iota(jnp.int32, (R, R), 0) >= lax.broadcasted_iota(jnp.int32, (R, R), 1)
    inverse_high, inverse_low = split(jnp.where(lower, a[...] * math.sqrt(D), 0.0))
    arrive(pairs)

    def dot(p, q):
        return jnp.dot(p, q, preferred_element_type=jnp.float32)

    for c in range(2):
        for p in range(2):
            for q in range(0, 4, 2):
                block = jnp.concatenate([rows[c, p, q].reshape(R, 128), rows[c, p, q + 1].reshape(R, 128)], axis=1)
                high, low = split(block)
                product = dot(inverse_high, high) + (dot(inverse_high, low) + dot(inverse_low, high))
                first = p * 512 + q * 128
                basis_t[c, :, first:first + 256] = product.astype(jnp.bfloat16)
    coef_copies = []
    for piece, (first, width) in enumerate(PIECES):
        product = jnp.zeros((R, width), jnp.float32)
        for c in range(2):
            product = product + lax.dot_general(
                basis_t[c], w_ref[c, first:first + width, :], NT, preferred_element_type=jnp.float32)
        product = product.reshape(4, 64, width)
        coef[:, :, first:first + width] = product
        coef_send[:, :, first:first + width] = product.astype(jnp.bfloat16)
        lanes = pl.ds(first, width if piece < 2 else PAD - first)
        coef_copies.append([
            send(coef_send.at[x_of(k), :, lanes], coef_in.at[k - 1, :, lanes], c_ss.at[piece, k - 1],
                 c_rs.at[piece, k - 1], {"row": x_of(k)})
            for k in (2, 1, 3)])
    for c in range(2):
        for q in range(4):
            first = c * 1024 + q * 256
            basis_out[first:first + 256, :] = basis_t[c, :, q * 256:q * 256 + 256].T
    for piece, (first, width) in enumerate(PIECES):
        arrive(coef_copies[piece])
        total = coef[row, :, first:first + width]
        for k in range(3):
            total = total + coef_in[k, :, first:first + width].astype(jnp.float32)
        coef_out[:, first:first + width] = total / math.sqrt(D)
    for copy in sent:
        copy.wait_send()


def shards(weights, sketch):
    f32, bf16, dma = jnp.float32, jnp.bfloat16, pltpu.SemaphoreType.DMA
    vmem = pl.BlockSpec(memory_space=pltpu.VMEM)
    return pl.pallas_call(
        whole,
        out_shape=(pltpu.VMEM((2048, R), bf16), pltpu.VMEM((64, WIDTH), f32)),
        in_specs=[pl.BlockSpec(memory_space=pltpu.HBM)] * 2,
        out_specs=(vmem, vmem),
        scratch_shapes=[
            pltpu.VMEM((2, WIDTH, 1024), bf16),
            pltpu.VMEM((WIDTH, R), bf16),
            pltpu.VMEM((R, WIDTH), bf16),
            pltpu.VMEM((2, 2, 4, 16, 2, 8, 128), f32),
            pltpu.VMEM((2, 2, 4, 16, 8, 128), f32),
            pltpu.VMEM((2, 2, 4, 16, 8, 128), f32),
            pltpu.VMEM((2, 2, 3, 16, 8, 128), f32),
            pltpu.VMEM((2, 2, 16, 8, 128), f32),
            pltpu.VMEM((2, 2, 15, 8, 128), f32),
            pltpu.VMEM((2, 2, 4, 16, 2, 8, 128), f32),
            pltpu.VMEM((4, 8, 8, R), f32),
            pltpu.VMEM((31, 8, R), f32),
            pltpu.VMEM((4, 8, 8, R), f32),
            pltpu.VMEM((R, R), f32),
            pltpu.VMEM((R, 3 * PANEL), bf16),
            pltpu.VMEM((3 * PANEL, R), bf16),
            pltpu.VMEM((2, R, 1024), bf16),
            pltpu.VMEM((4, 64, WIDTH), f32),
            pltpu.VMEM((4, 64, PAD), bf16),
            pltpu.VMEM((3, 64, PAD), bf16),
            dma((3,)), dma((2, 2)), dma((2, 2)), dma((2, 2, 3)), dma((2, 2, 3)), dma((2, 2, 15)), dma((2, 2, 15)),
            dma((2, 2, 15)), dma((2, 2, 15)), dma((2, 3)), dma((2, 3)), dma((2,)), dma((2,)),
            dma((31,)), dma((31,)), dma((31,)), dma((31,)), dma((4, 3)), dma((4, 3)),
        ],
        compiler_params=pltpu.CompilerParams(
            collective_id=0, has_side_effects=True, vmem_limit_bytes=54 << 20),
    )(weights.T, sketch)


def solution(mesh):
    placed = (P("row", ("section", "col")), P(("section", "col"), None))
    return jax.shard_map(
        shards,
        mesh=mesh,
        in_specs=placed,
        out_specs=(P("row", None), P("row", ("section", "col"))),
        check_vma=False,
    )
```

```python
import math

import jax
import jax.numpy as jnp
from jax import lax
from jax.experimental import pallas as pl
from jax.experimental.pallas import tpu as pltpu
from jax.sharding import PartitionSpec as P

D = 8192
R = 256
WIDTH = 832
PAD = 896
PANEL = 64
PIECES = ((0, 512), (512, 320))
QUARTERS = ((0, 0), (0, 1), (1, 0), (1, 1))
GROUP = tuple(sorted(range(1, 32), key=lambda k: -(2 * min(k // 8, 4 - k // 8) + min(k % 8, 8 - k % 8))))
FAR_FIRST = (8, 7, 9, 6, 10, 5, 11, 4, 12, 3, 13, 2, 14, 1, 15)
MESH = pl.DeviceIdType.MESH
NT = (((1,), (1,)), ((), ()))


def split(x):
    high = x.astype(jnp.bfloat16)
    return high, (x - high.astype(jnp.float32)).astype(jnp.bfloat16)


def spread_lane(x, lane):
    return jnp.take_along_axis(x, jnp.full((8, 128), lane, jnp.int32), axis=1)


def factor_half(half, a, left, right):
    lane = lax.broadcasted_iota(jnp.int32, (8, 128), 1)
    sub = lax.broadcasted_iota(jnp.int32, (8, 128), 0)
    lane256 = lax.broadcasted_iota(jnp.int32, (PANEL, R), 1)
    sub256 = lax.broadcasted_iota(jnp.int32, (PANEL, R), 0)
    lanes = lax.broadcasted_iota(jnp.int32, (R, R), 1)
    subs = lax.broadcasted_iota(jnp.int32, (R, R), 0)
    groups = PANEL // 8
    mine, rest = slice(half * 128, half * 128 + 128), slice((1 - half) * 128, (1 - half) * 128 + 128)

    @pl.loop(0, 128 // PANEL)
    def _(q):
        base = half * 128 + q * PANEL
        rows = pl.ds(pl.multiple_of(base, PANEL), PANEL)
        factors = right[...]
        panel = jnp.where((lane256 >= base - PANEL) & (lane256 < base), 0.0, a[rows, :]) - jnp.dot(
            left[rows, :], factors, preferred_element_type=jnp.float32)
        old = (lanes >= base - PANEL) & (lanes < base) & (subs >= base)
        below = jnp.where(old, 0.0, a[...]) - jnp.dot(left[...], factors, preferred_element_type=jnp.float32)
        x = [panel[8 * g:8 * g + 8, mine] for g in range(groups)]
        z = [panel[8 * g:8 * g + 8, rest] for g in range(groups)]
        for b in range(groups):
            lane0 = q * PANEL + 8 * b
            inside = (lane >= lane0) & (lane < lane0 + 8)
            columns = {g: [spread_lane(x[g], lane0 + j) for j in range(8)] for g in range(b, groups)}
            s = {}
            for j in range(8):
                for i in range(j, 8):
                    s[i, j] = jnp.broadcast_to(columns[b][j][i:i + 1, :], (8, 128))
            u, v = [], []
            for i in range(8):
                spread = jnp.broadcast_to(x[b][i:i + 1, :], (8, 128))
                u.append(jnp.where(inside, jnp.where(lane == lane0 + i, 1.0, 0.0), spread))
                v.append(jnp.broadcast_to(z[b][i:i + 1, :], (8, 128)))
            for g in range(b + 1, groups):
                x[g] = jnp.where(inside, 0.0, x[g])
            for j in range(8):
                scale = lax.rsqrt(s[j, j])
                for i in range(j + 1, 8):
                    s[i, j] = s[i, j] * scale
                for i in range(j + 1, 8):
                    for k in range(j + 1, i + 1):
                        s[i, k] = s[i, k] - s[i, j] * s[k, j]
                u[j] = u[j] * scale
                v[j] = v[j] * scale
                for i in range(j + 1, 8):
                    u[i] = u[i] - s[i, j] * u[j]
                    v[i] = v[i] - s[i, j] * v[j]
                for g in range(b + 1, groups):
                    multiplier = columns[g][j] * scale
                    for k in range(j + 1, 8):
                        columns[g][k] = columns[g][k] - multiplier * s[k, j]
                    x[g] = x[g] - multiplier * u[j]
                    z[g] = z[g] - multiplier * v[j]
            x[b], z[b] = u[0], v[0]
            for i in range(1, 8):
                x[b] = jnp.where(sub == i, u[i], x[b])
                z[b] = jnp.where(sub == i, v[i], z[b])
        parts = [jnp.concatenate(x, axis=0), jnp.concatenate(z, axis=0)]
        new = jnp.concatenate(parts if half == 0 else parts[::-1], axis=1)
        a[...] = below
        a[rows, :] = new
        high, low = split(jnp.where((lane256 > base + sub256) & (lane256 < base + PANEL), 0.0, new))
        right[0:PANEL, :] = high
        right[PANEL:2 * PANEL, :] = low
        right[2 * PANEL:, :] = high
        high, low = split(jnp.where(lane256 >= base + PANEL, new, 0.0).T)
        left[:, 0:PANEL] = high
        left[:, PANEL:2 * PANEL] = high
        left[:, 2 * PANEL:] = low


def whole(w_hbm, s_hbm, basis_out, coef_out, w_ref, s_ref, st_ref, part, core_in, core_sum, y_in, y_sum, z_in,
          rows, gram_part, gram_in, gram_all, a, left, right, basis_t, coef, coef_send, coef_in,
          w_sem, core_ss, core_rs, y_ss, y_rs, z_ss, z_rs, h_ss, h_rs, hy_ss, hy_rs, hc_ss, hc_rs,
          g_ss, g_rs, b_ss, b_rs, c_ss, c_rs):
    section = lax.axis_index("section")
    row = lax.axis_index("row")
    col = lax.axis_index("col")
    core = lax.rem(section, 2)
    y = section // 2
    other = 1 - core
    sibling = {"section": 2 * y + other}

    def y_of(k):
        return lax.rem(y + k, 4)

    def z_of(k):
        return lax.rem(col + k, 16)

    def x_of(k):
        return lax.rem(row + k, 4)

    def to_y(k):
        return {"section": 2 * y_of(k) + core}

    def to_z(k):
        return {"col": z_of(k)}

    def group_of(k):
        return lax.rem(row + k // 8, 4), lax.rem(section + k % 8, 8)

    def to_group(k):
        r, s = group_of(k)
        return {"row": r, "section": s}

    sent, pending = [], []

    def send(src, dst, ss, rs, device):
        copy = pltpu.make_async_remote_copy(
            src_ref=src, dst_ref=dst, send_sem=ss, recv_sem=rs, device_id=device, device_id_type=MESH)
        copy.start()
        sent.append(copy)
        pending.append(copy)
        return copy

    def arrive(copies):
        for copy in copies:
            copy.wait_recv()
            pending[:] = [c for c in pending if c is not copy]

    barrier = pltpu.get_barrier_semaphore()
    for k in range(1, 32):
        pl.semaphore_signal(barrier, inc=1, device_id=to_group(k), device_id_type=MESH)
    for k in range(1, 16):
        pl.semaphore_signal(barrier, inc=1, device_id=to_z(k), device_id_type=MESH)

    loads, core_copies = [], []
    load_s = pltpu.make_async_copy(s_hbm, s_ref, w_sem.at[4])
    load_s.start()
    halves = (other, core)
    for half in range(2):
        for p in range(2):
            load = pltpu.make_async_copy(
                w_hbm.at[:, pl.ds(pl.multiple_of(halves[half] * 1024 + p * 512, 512), 512)],
                w_ref.at[halves[half], :, pl.ds(p * 512, 512)], w_sem.at[2 * half + p])
            load.start()
            loads.append(load)

    load_s.wait()
    st_ref[...] = s_ref[...].T

    def multiply(half, p):
        loads[2 * half + p].wait()
        product = jnp.dot(
            st_ref[...], w_ref[halves[half], :, p * 512:p * 512 + 512], preferred_element_type=jnp.float32)
        for q in range(4):
            part[half, p, q] = product[:, q * 128:q * 128 + 128].reshape(16, 2, 8, 128)

    for p in range(2):
        multiply(0, p)
        if p == 0:
            pl.semaphore_wait(barrier, 46)
        core_copies += [
            send(part.at[0, p, :, :, r], core_in.at[p, r], core_ss.at[p, r], core_rs.at[p, r], sibling)
            for r in range(2)]
    y_copies = []
    for quarter, (p, r) in enumerate(QUARTERS):
        if r == 0:
            multiply(1, p)
        arrive([core_copies[quarter]])
        core_sum[p, r] = part[1, p, :, :, r] + core_in[p, r]
        y_copies.append([
            send(core_sum.at[p, r, y_of(k)], y_in.at[p, r, k - 1], y_ss.at[p, r, k - 1], y_rs.at[p, r, k - 1], to_y(k))
            for k in (2, 1, 3)])
    z_copies = []
    for quarter, (p, r) in enumerate(QUARTERS):
        arrive(y_copies[quarter])
        y_sum[p, r] = core_sum[p, r, y] + y_in[p, r, 0] + y_in[p, r, 1] + y_in[p, r, 2]
        z_copies.append([
            send(y_sum.at[p, r, z_of(k)], z_in.at[p, r, k - 1], z_ss.at[p, r, k - 1], z_rs.at[p, r, k - 1], to_z(k))
            for k in FAR_FIRST])
    gathers = []
    for quarter, (p, r) in enumerate(QUARTERS):
        arrive(z_copies[quarter])
        total = y_sum[p, r, col]
        for k in range(15):
            total = total + z_in[p, r, k]
        rows[core, p, y, col, r] = total
        gathers.append([
            send(rows.at[core, p, y, col, r], rows.at[core, p, y, col, r], h_ss.at[p, r, k - 1], h_rs.at[p, r, k - 1],
                 to_z(k))
            for k in FAR_FIRST])

    def spread(p):
        return [
            send(rows.at[core, p, y], rows.at[core, p, y], hy_ss.at[p, k - 1], hy_rs.at[p, k - 1], to_y(k))
            for k in (2, 1, 3)]

    def pair(p):
        return send(rows.at[core, p], rows.at[core, p], hc_ss.at[p], hc_rs.at[p], sibling)

    gram = jnp.zeros((R, R), jnp.float32)
    spreads = []
    for p in range(2):
        arrive(gathers[2 * p])
        arrive(gathers[2 * p + 1])
        if p == 0:
            spreads.append(spread(0))
        high, low = split(rows[core, p, y].reshape(R, 128))
        gram = gram + (lax.dot_general(high, high, NT, preferred_element_type=jnp.float32) + (
            lax.dot_general(high, low, NT, preferred_element_type=jnp.float32) +
            lax.dot_general(low, high, NT, preferred_element_type=jnp.float32)))
    gram_part[...] = gram.reshape(4, 8, 8, R)
    gram_copies = {}
    for k in GROUP:
        r, s = group_of(k)
        gram_copies[k] = send(gram_part.at[r, s], gram_in.at[k - 1], g_ss.at[k - 1], g_rs.at[k - 1], to_group(k))
    total = gram_part[row, section]
    for k in GROUP[::-1]:
        arrive([gram_copies[k]])
        total = total + gram_in[k - 1]
    gram_all[row, section] = total
    back_copies = [
        send(gram_all.at[row, section], gram_all.at[row, section], b_ss.at[k - 1], b_rs.at[k - 1], to_group(k))
        for k in GROUP]
    spreads.append(spread(1))
    coef_send[:, :, 768:] = jnp.zeros((4, 64, PAD - 768), jnp.bfloat16)
    left[...] = jnp.zeros_like(left)
    right[...] = jnp.zeros_like(right)
    arrive(spreads[0])
    pairs = [pair(0)]
    arrive(back_copies)
    a[...] = gram_all[...].reshape(R, R)
    factor_half(0, a, left, right)
    arrive(spreads[1])
    pairs.append(pair(1))
    factor_half(1, a, left, right)

    lower = lax.broadcasted_iota(jnp.int32, (R, R), 0) >= lax.broadcasted_iota(jnp.int32, (R, R), 1)
    inverse_high, inverse_low = split(jnp.where(lower, a[...] * math.sqrt(D), 0.0))
    arrive(pairs)

    def dot(p, q):
        return jnp.dot(p, q, preferred_element_type=jnp.float32)

    for c in range(2):
        for p in range(2):
            for q in range(0, 4, 2):
                block = jnp.concatenate([rows[c, p, q].reshape(R, 128), rows[c, p, q + 1].reshape(R, 128)], axis=1)
                high, low = split(block)
                product = dot(inverse_high, high) + (dot(inverse_high, low) + dot(inverse_low, high))
                first = p * 512 + q * 128
                basis_t[c, :, first:first + 256] = product.astype(jnp.bfloat16)
    coef_copies = []
    for piece, (first, width) in enumerate(PIECES):
        product = jnp.zeros((R, width), jnp.float32)
        for c in range(2):
            product = product + lax.dot_general(
                basis_t[c], w_ref[c, first:first + width, :], NT, preferred_element_type=jnp.float32)
        product = product.reshape(4, 64, width)
        coef[:, :, first:first + width] = product
        coef_send[:, :, first:first + width] = product.astype(jnp.bfloat16)
        lanes = pl.ds(first, width if piece < 1 else PAD - first)
        coef_copies.append([
            send(coef_send.at[x_of(k), :, lanes], coef_in.at[k - 1, :, lanes], c_ss.at[piece, k - 1],
                 c_rs.at[piece, k - 1], {"row": x_of(k)})
            for k in (2, 1, 3)])
    for c in range(2):
        for q in range(4):
            first = c * 1024 + q * 256
            basis_out[first:first + 256, :] = basis_t[c, :, q * 256:q * 256 + 256].T
    for piece, (first, width) in enumerate(PIECES):
        arrive(coef_copies[piece])
        total = coef[row, :, first:first + width]
        for k in range(3):
            total = total + coef_in[k, :, first:first + width].astype(jnp.float32)
        coef_out[:, first:first + width] = total / math.sqrt(D)
    for copy in sent:
        copy.wait_send()


def shards(weights, sketch):
    f32, bf16, dma = jnp.float32, jnp.bfloat16, pltpu.SemaphoreType.DMA
    vmem = pl.BlockSpec(memory_space=pltpu.VMEM)
    return pl.pallas_call(
        whole,
        out_shape=(pltpu.VMEM((2048, R), bf16), pltpu.VMEM((64, WIDTH), f32)),
        in_specs=[pl.BlockSpec(memory_space=pltpu.HBM)] * 2,
        out_specs=(vmem, vmem),
        scratch_shapes=[
            pltpu.VMEM((2, WIDTH, 1024), bf16),
            pltpu.VMEM((WIDTH, R), bf16),
            pltpu.VMEM((R, WIDTH), bf16),
            pltpu.VMEM((2, 2, 4, 16, 2, 8, 128), f32),
            pltpu.VMEM((2, 2, 4, 16, 8, 128), f32),
            pltpu.VMEM((2, 2, 4, 16, 8, 128), f32),
            pltpu.VMEM((2, 2, 3, 16, 8, 128), f32),
            pltpu.VMEM((2, 2, 16, 8, 128), f32),
            pltpu.VMEM((2, 2, 15, 8, 128), f32),
            pltpu.VMEM((2, 2, 4, 16, 2, 8, 128), f32),
            pltpu.VMEM((4, 8, 8, R), f32),
            pltpu.VMEM((31, 8, R), f32),
            pltpu.VMEM((4, 8, 8, R), f32),
            pltpu.VMEM((R, R), f32),
            pltpu.VMEM((R, 3 * PANEL), bf16),
            pltpu.VMEM((3 * PANEL, R), bf16),
            pltpu.VMEM((2, R, 1024), bf16),
            pltpu.VMEM((4, 64, WIDTH), f32),
            pltpu.VMEM((4, 64, PAD), bf16),
            pltpu.VMEM((3, 64, PAD), bf16),
            dma((5,)), dma((2, 2)), dma((2, 2)), dma((2, 2, 3)), dma((2, 2, 3)), dma((2, 2, 15)), dma((2, 2, 15)),
            dma((2, 2, 15)), dma((2, 2, 15)), dma((2, 3)), dma((2, 3)), dma((2,)), dma((2,)),
            dma((31,)), dma((31,)), dma((31,)), dma((31,)), dma((4, 3)), dma((4, 3)),
        ],
        compiler_params=pltpu.CompilerParams(
            collective_id=0, has_side_effects=True, vmem_limit_bytes=54 << 20),
    )(weights.T, sketch)


def solution(mesh):
    placed = (P("row", ("section", "col")), P(("section", "col"), None))
    return jax.shard_map(
        shards,
        mesh=mesh,
        in_specs=placed,
        out_specs=(P("row", None), P("row", ("section", "col"))),
        check_vma=False,
    )
```
